512 devices in a mesh: ha: 8 (over y), wa: 16 (over z, x_hi), fsdp: 4 (over x_lo, core).
Axes of the slice: x: 4 (x_hi: 2, x_lo: 2; x = x_hi * 2 + x_lo), y: 8, z: 8, core: 2. Of those that a mesh axis runs over, the one named last changes fastest.
Arguments:
- latent: bfloat16 [4, 1, 128, 128, 1536], P('fsdp', None, 'ha', 'wa'), may hold values from -6 to 6
- qkv_weight: bfloat16 [1536, 12, 384], P(None, 'fsdp'), may hold values from -0.15625 to 0.15625
- query_gain: float32 [128], replicated, may hold values from 0.1 to 1.9
- key_gain: float32 [128], replicated, may hold values from 0.1 to 1.9
Outputs:
- attended: bfloat16 [4, 1, 128, 128, 1536], P('fsdp', None, 'ha', 'wa')
The draws below stay inside these ranges and needn't reach their ends.
All inputs are finite; a program needn't handle non-finite values.
Results may differ from the reference program's by a relative error of at most 0.011.
Values may be sent and summed in bfloat16 or wider, within the bound.
A program may use at most 64 MiB of HBM per device.

```python
import math
import jax
import jax.numpy as jnp
from jax import lax

D = 1536
HEADS = 12
HD = 128
WIN = 8
FRAMES = 1
ROWS = 128
COLS = 128
BATCH = 4


def shard_levels(own_key, shape, split, low, high):
    level = 1.0
    for axis_at, blocks in split:
        heights = jax.random.uniform(jax.random.fold_in(jax.random.fold_in(own_key, 6), axis_at), (blocks,), jnp.float32, low / len(split), high / len(split))
        level = level * jnp.repeat(jnp.exp(heights), shape[axis_at] // blocks).reshape((-1,) + (1,) * (len(shape) - 1 - axis_at))
    return level


def normal_values(own_key, shape, scale, bound, cuts=(), kind=jnp.bfloat16):
    level = shard_levels(own_key, shape, cuts, -0.22, 0.18) if cuts else 1.0
    values = jax.random.normal(own_key, shape, jnp.float32) * scale * level
    return jnp.minimum(jnp.maximum(values, -bound), bound).astype(kind)


def setup_inputs(seed: int = 0) -> dict:
    arg_keys = jax.random.split(jax.random.key(seed), 5)
    return {
        "latent": normal_values(arg_keys[0], (BATCH, FRAMES, ROWS, COLS, D), 1.0, 6.0, ((0, 4), (2, 8), (3, 16))),
        "qkv_weight": normal_values(arg_keys[1], (D, HEADS, 3 * HD), D ** -0.5, 0.15625, ((1, 4),)),
        "query_gain": jnp.clip(1.0 + 0.18 * jax.random.normal(arg_keys[2], (HD,), jnp.float32), 0.1, 1.9),
        "key_gain": jnp.clip(1.0 + 0.18 * jax.random.normal(arg_keys[3], (HD,), jnp.float32), 0.1, 1.9),
    }


def rms_gain(part, gain):
    values32 = part.astype(jnp.float32)
    scale = lax.rsqrt(lax.optimization_barrier(jnp.mean(values32 * values32, axis=-1, keepdims=True)) + 1e-06)
    return (values32 * scale * gain).astype(jnp.bfloat16)

def to_windows(array):
    shaped = array.reshape(FRAMES, ROWS // WIN, WIN, COLS // WIN, WIN, HEADS, HD)
    shaped = shaped.transpose(1, 3, 5, 0, 2, 4, 6)
    return shaped.reshape(ROWS // WIN, COLS // WIN, HEADS, FRAMES * WIN * WIN, HD)

def reference(latent, qkv_weight, query_gain, key_gain):
    half_win = WIN // 2

    def one_clip(sample):
        token_rows = sample.reshape(-1, D)
        packed = jnp.dot(token_rows, qkv_weight.reshape(D, HEADS * 3 * HD), preferred_element_type=jnp.float32)
        packed = packed.astype(jnp.bfloat16).reshape(FRAMES, ROWS, COLS, HEADS, 3 * HD)
        queries = rms_gain(packed[..., :HD], query_gain)
        keyed = rms_gain(packed[..., HD:2 * HD], key_gain)
        valued = packed[..., 2 * HD:]
        queries = jnp.roll(queries, (-half_win, -half_win), axis=(1, 2))
        keyed = jnp.roll(keyed, (-half_win, -half_win), axis=(1, 2))
        valued = jnp.roll(valued, (-half_win, -half_win), axis=(1, 2))
        query_win = to_windows(queries).astype(jnp.float32)
        key_win = to_windows(keyed).astype(jnp.float32)
        value_win = to_windows(valued).astype(jnp.float32)
        scores = jnp.einsum('abhqe,abhke->abhqk', query_win, key_win, precision=lax.Precision.HIGHEST) / math.sqrt(HD)
        probs = jax.nn.softmax(scores, axis=-1).astype(jnp.bfloat16)
        output = jnp.einsum('abhqk,abhke->abhqe', probs.astype(jnp.float32), value_win, precision=lax.Precision.HIGHEST)
        output = output.astype(jnp.bfloat16)
        output = output.reshape(ROWS // WIN, COLS // WIN, HEADS, FRAMES, WIN, WIN, HD)
        output = output.transpose(3, 0, 4, 1, 5, 2, 6).reshape(FRAMES, ROWS, COLS, HEADS * HD)
        return jnp.roll(output, (half_win, half_win), axis=(1, 2))
    return lax.map(one_clip, latent)
```

```python
import math

import jax
import jax.numpy as jnp
from jax import lax
from jax.experimental import pallas as pl
from jax.experimental.pallas import tpu as pltpu
from jax.sharding import PartitionSpec as P

MESH = pl.DeviceIdType.MESH
HEAD = 128
HALF = 4
LOCAL_HEADS = 3
GROUP = LOCAL_HEADS * HEAD
ROWS = 16
COLS = 8
TOKENS = ROWS * COLS
DEPTH = 1536
PIECES = ((0, 48, 0, 0), (48, 16, 1, 0), (64, 48, 0, 1), (112, 16, 1, 1))


def token_of(place):
    half, rest = place // 64, place % 64
    row = (rest // 4 + HALF) % ROWS
    return row * COLS + rest % 4 + HALF * (1 - half)


def normalized(part, gain):
    values = part.astype(jnp.float32)
    scale = lax.rsqrt(jnp.mean(values * values, axis=-1, keepdims=True) + 1e-06)
    return (values * scale * gain).astype(jnp.bfloat16)


def kernel(
    latent_hbm, weight_hbm, query_gain, key_gain, out_ref,
    latent, weight, sending, tile, blended, stage,
    load_sems, send_in, recv_in, send_twin, recv_twin, send_out, recv_out,
):
    h, w, s = lax.axis_index("ha"), lax.axis_index("wa"), lax.axis_index("fsdp")
    h_size, w_size = lax.axis_size("ha"), lax.axis_size("wa")

    def device(back_h, back_w, other):
        group = s
        if other & 1:
            group = group + 1 - 2 * lax.rem(group, 2)
        if other & 2:
            group = lax.rem(group + 2, 4)
        return (lax.rem(h - back_h + h_size, h_size), lax.rem(w - back_w + w_size, w_size), group)

    load_latent = pltpu.make_async_copy(latent_hbm, latent, load_sems.at[0])
    load_latent.start()
    load_weight = pltpu.make_async_copy(weight_hbm, weight, load_sems.at[1])
    load_weight.start()

    barrier = pltpu.get_barrier_semaphore()
    partners = [
        device(back_h, back_w, other)
        for back_h, back_w in ((0, 0), (1, 0), (0, 1), (1, 1), (-1, 0), (0, -1), (-1, -1))
        for other in range(4)
        if (back_h, back_w, other) != (0, 0, 0)
    ]
    for partner in partners:
        pl.semaphore_signal(barrier, inc=1, device_id=partner, device_id_type=MESH)

    place = lax.broadcasted_iota(jnp.int32, (TOKENS, TOKENS), 0)
    token = lax.broadcasted_iota(jnp.int32, (TOKENS, TOKENS), 1)
    arrange = jnp.where(token_of(place) == token, 1.0, 0.0).astype(jnp.bfloat16)
    place = lax.broadcasted_iota(jnp.int32, (TOKENS, TOKENS), 1)
    token = lax.broadcasted_iota(jnp.int32, (TOKENS, TOKENS), 0)
    restore = jnp.where(token_of(place) == token, 1.0, 0.0).astype(jnp.bfloat16)

    load_latent.wait()
    mine = latent[...].astype(jnp.float32).reshape(TOKENS, DEPTH).astype(jnp.bfloat16)
    sending[...] = jnp.dot(arrange, mine, preferred_element_type=jnp.float32).astype(jnp.bfloat16)
    tile[0, pl.ds(0, 48)] = sending[pl.ds(0, 48)]

    pl.semaphore_wait(barrier, len(partners))

    incoming = {}
    for slot in (0, 2):
        for index, (first, rows, back_h, back_w) in enumerate(PIECES):
            if slot == 0 and index == 0:
                continue
            at = slot * 2 + index
            copy = pltpu.make_async_remote_copy(
                src_ref=sending.at[pl.ds(first, rows)],
                dst_ref=tile.at[slot, pl.ds(first, rows)],
                send_sem=send_in.at[at],
                recv_sem=recv_in.at[at],
                device_id=device(back_h, back_w, slot),
                device_id_type=MESH,
            )
            copy.start()
            incoming[slot, index] = copy

    twin = {}

    def forward(slot, index):
        first, rows = PIECES[index][:2]
        at = slot * 2 + index
        copy = pltpu.make_async_remote_copy(
            src_ref=tile.at[slot, pl.ds(first, rows)],
            dst_ref=tile.at[slot + 1, pl.ds(first, rows)],
            send_sem=send_twin.at[at],
            recv_sem=recv_twin.at[at],
            device_id=device(0, 0, 1),
            device_id_type=MESH,
        )
        copy.start()
        twin[slot, index] = copy

    def gather(slot):
        for index in range(4):
            if (slot, index) in incoming:
                incoming[slot, index].wait_recv()
            forward(slot, index)
        for index in range(4):
            twin[slot, index].wait_recv()

    spot_q = lax.broadcasted_iota(jnp.int32, (TOKENS, TOKENS), 0)
    spot_k = lax.broadcasted_iota(jnp.int32, (TOKENS, TOKENS), 1)
    together = (spot_q % 64 < 32) == (spot_k % 64 < 32)

    outgoing = {}

    def attend(slot):
        tokens = jnp.concatenate([tile[slot], tile[slot + 1]], axis=0)
        for head in range(LOCAL_HEADS):
            packed = jnp.dot(tokens, weight[head], preferred_element_type=jnp.float32).astype(jnp.bfloat16)
            queries = normalized(packed[:, :HEAD], query_gain[...])
            keyed = normalized(packed[:, HEAD : 2 * HEAD], key_gain[...])
            valued = packed[:, 2 * HEAD :]
            for clip in range(2):
                at = slice(clip * TOKENS, (clip + 1) * TOKENS)
                scores = lax.dot_general(
                    queries[at], keyed[at], (((1,), (1,)), ((), ())), preferred_element_type=jnp.float32
                ) * (1.0 / math.sqrt(HEAD))
                scores = jnp.where(together, scores, -1e30)
                raised = jnp.exp(scores - jnp.max(scores, axis=-1, keepdims=True))
                probs = (raised / jnp.sum(raised, axis=-1, keepdims=True)).astype(jnp.bfloat16)
                result = jnp.dot(probs, valued[at], preferred_element_type=jnp.float32)
                blended[slot + clip, :, pl.ds(head * HEAD, HEAD)] = result.astype(jnp.bfloat16)
        for clip in (slot, slot + 1):
            for index, (first, rows, back_h, back_w) in enumerate(PIECES):
                if clip == 0 and index == 0:
                    stage[0, pl.ds(0, 48)] = blended[0, pl.ds(0, 48)]
                    continue
                at = clip * 4 + index
                copy = pltpu.make_async_remote_copy(
                    src_ref=blended.at[clip, pl.ds(first, rows)],
                    dst_ref=stage.at[clip, pl.ds(first, rows)],
                    send_sem=send_out.at[at],
                    recv_sem=recv_out.at[at],
                    device_id=device(-back_h, -back_w, clip),
                    device_id_type=MESH,
                )
                copy.start()
                outgoing[clip, index] = copy

    gather(0)
    load_weight.wait()
    attend(0)
    gather(2)
    attend(2)

    for clip in range(4):
        for index in range(4):
            if (clip, index) in outgoing:
                outgoing[clip, index].wait_recv()
        group = device(0, 0, clip)[2]
        columns = pl.ds(pl.multiple_of(group * GROUP, GROUP), GROUP)
        out_ref[:, columns] = jnp.dot(restore, stage[clip], preferred_element_type=jnp.float32).astype(jnp.bfloat16)
    for copy in [*incoming.values(), *twin.values(), *outgoing.values()]:
        copy.wait_send()


def shards(latent, qkv_weight, query_gain, key_gain):
    vmem = pl.BlockSpec(memory_space=pltpu.VMEM)
    anywhere = pl.BlockSpec(memory_space=pl.ANY)
    out = pl.pallas_call(
        kernel,
        out_shape=jax.ShapeDtypeStruct((TOKENS, DEPTH), jnp.bfloat16),
        in_specs=[anywhere, anywhere, vmem, vmem],
        out_specs=vmem,
        scratch_shapes=[
            pltpu.VMEM((ROWS, COLS, DEPTH), jnp.bfloat16),
            pltpu.VMEM((LOCAL_HEADS, DEPTH, GROUP), jnp.bfloat16),
            pltpu.VMEM((TOKENS, DEPTH), jnp.bfloat16),
            pltpu.VMEM((4, TOKENS, DEPTH), jnp.bfloat16),
            pltpu.VMEM((4, TOKENS, GROUP), jnp.bfloat16),
            pltpu.VMEM((4, TOKENS, GROUP), jnp.bfloat16),
            pltpu.SemaphoreType.DMA((2,)),
            pltpu.SemaphoreType.DMA((8,)),
            pltpu.SemaphoreType.DMA((8,)),
            pltpu.SemaphoreType.DMA((8,)),
            pltpu.SemaphoreType.DMA((8,)),
            pltpu.SemaphoreType.DMA((16,)),
            pltpu.SemaphoreType.DMA((16,)),
        ],
        compiler_params=pltpu.CompilerParams(
            collective_id=0, has_side_effects=True, vmem_limit_bytes=60 * 1024 * 1024
        ),
    )(
        latent.reshape(ROWS, COLS, DEPTH),
        qkv_weight.transpose(1, 0, 2),
        query_gain.reshape(1, HEAD),
        key_gain.reshape(1, HEAD),
    )
    return out.reshape(latent.shape)


def solution(mesh):
    return jax.shard_map(
        shards,
        mesh=mesh,
        in_specs=(P("fsdp", None, "ha", "wa", None), P(None, "fsdp", None), P(), P()),
        out_specs=P("fsdp", None, "ha", "wa", None),
        check_vma=False,
    )
```

```python
import math

import jax
import jax.numpy as jnp
from jax import lax
from jax.experimental import pallas as pl
from jax.experimental.pallas import tpu as pltpu
from jax.sharding import PartitionSpec as P

MESH = pl.DeviceIdType.MESH
HEAD = 128
HALF = 4
LOCAL_HEADS = 3
GROUP = LOCAL_HEADS * HEAD
ROWS = 16
COLS = 8
TOKENS = ROWS * COLS
DEPTH = 1536
PIECES = ((0, 48, 0, 1), (48, 16, -1, 1), (64, 48, 0, 0), (112, 16, -1, 0))
STAYS = 2


def token_of(place):
    half, rest = place // 64, place % 64
    row = (rest // 4 + HALF) % ROWS
    return row * COLS + rest % 4 + HALF * (1 - half)


def normalized(part, gain):
    values = part.astype(jnp.float32)
    scale = lax.rsqrt(jnp.mean(values * values, axis=-1, keepdims=True) + 1e-06)
    return (values * scale * gain).astype(jnp.bfloat16)


def kernel(
    latent_hbm, weight_hbm, query_gain_hbm, key_gain_hbm, out_ref,
    latent, weight, query_gain, key_gain, sending, tile, blended, stage,
    load_sems, send_in, recv_in, send_twin, recv_twin, send_out, recv_out,
):
    h, w, s = lax.axis_index("ha"), lax.axis_index("wa"), lax.axis_index("fsdp")
    h_size, w_size = lax.axis_size("ha"), lax.axis_size("wa")

    def device(on_h, on_w, other):
        group = s
        if other & 1:
            group = group + 1 - 2 * lax.rem(group, 2)
        if other & 2:
            group = lax.rem(group + 2, 4)
        return (lax.rem(h + on_h + h_size, h_size), lax.rem(w + on_w + w_size, w_size), group)

    barrier = pltpu.get_barrier_semaphore()
    givers = [device(0, 0, 1)]
    for slot in (0, 2):
        for index, (_, _, on_h, on_w) in enumerate(PIECES):
            if (slot, index) != (0, STAYS):
                givers.append(device(-on_h, -on_w, slot))
    for giver in givers:
        pl.semaphore_signal(barrier, inc=1, device_id=giver, device_id_type=MESH)

    load_latent = pltpu.make_async_copy(latent_hbm, latent, load_sems.at[0])
    load_latent.start()
    loads = [
        pltpu.make_async_copy(source, target, load_sems.at[1 + at])
        for at, (source, target) in enumerate(
            ((query_gain_hbm, query_gain), (key_gain_hbm, key_gain), (weight_hbm, weight))
        )
    ]
    for load in loads:
        load.start()

    place = lax.broadcasted_iota(jnp.int32, (TOKENS, TOKENS), 0)
    token = lax.broadcasted_iota(jnp.int32, (TOKENS, TOKENS), 1)
    arrange = jnp.where(token_of(place) == token, 1.0, 0.0).astype(jnp.bfloat16)

    load_latent.wait()
    mine = latent[...].astype(jnp.float32).reshape(TOKENS, DEPTH).astype(jnp.bfloat16)
    sending[...] = jnp.dot(arrange, mine, preferred_element_type=jnp.float32).astype(jnp.bfloat16)

    pl.semaphore_wait(barrier, len(givers))

    incoming = {}
    for slot, index in ((0, 0), (0, 1), (2, 0), (2, 1), (0, 3), (2, 2), (2, 3)):
        first, rows, on_h, on_w = PIECES[index]
        at = slot * 2 + index
        copy = pltpu.make_async_remote_copy(
            src_ref=sending.at[pl.ds(first, rows)],
            dst_ref=tile.at[slot, pl.ds(first, rows)],
            send_sem=send_in.at[at],
            recv_sem=recv_in.at[at],
            device_id=device(on_h, on_w, slot),
            device_id_type=MESH,
        )
        copy.start()
        incoming[slot, index] = copy
    stays = pl.ds(PIECES[STAYS][0], PIECES[STAYS][1])
    tile[0, stays] = sending[stays]

    twin = {}

    def forward(slot):
        for index in (2, 3, 1, 0):
            first, rows = PIECES[index][:2]
            at = slot * 2 + index
            if (slot, index) in incoming:
                incoming[slot, index].wait_recv()
            copy = pltpu.make_async_remote_copy(
                src_ref=tile.at[slot, pl.ds(first, rows)],
                dst_ref=tile.at[slot + 1, pl.ds(first, rows)],
                send_sem=send_twin.at[at],
                recv_sem=recv_twin.at[at],
                device_id=device(0, 0, 1),
                device_id_type=MESH,
            )
            copy.start()
            twin[slot, index] = copy

    spot_q = lax.broadcasted_iota(jnp.int32, (TOKENS, TOKENS), 0)
    spot_k = lax.broadcasted_iota(jnp.int32, (TOKENS, TOKENS), 1)
    together = (spot_q % 64 < 32) == (spot_k % 64 < 32)

    outgoing = {}

    def attend(slot):
        tokens = tile[slot]
        for head in range(LOCAL_HEADS):
            packed = jnp.dot(tokens, weight[head], preferred_element_type=jnp.float32).astype(jnp.bfloat16)
            queries = normalized(packed[:, :HEAD], query_gain[...])
            keyed = normalized(packed[:, HEAD : 2 * HEAD], key_gain[...])
            scores = lax.dot_general(
                queries, keyed, (((1,), (1,)), ((), ())), preferred_element_type=jnp.float32
            ) * (1.0 / math.sqrt(HEAD))
            raised = jnp.exp(jnp.where(together, scores, -1e30))
            result = jnp.dot(
                raised.astype(jnp.bfloat16), packed[:, 2 * HEAD :], preferred_element_type=jnp.float32
            ) / jnp.sum(raised, axis=-1, keepdims=True)
            blended[slot, :, pl.ds(head * HEAD, HEAD)] = result.astype(jnp.bfloat16)
        for index, (first, rows, on_h, on_w) in enumerate(PIECES):
            if (slot, index) == (0, STAYS):
                stage[0, stays] = blended[0, stays]
                continue
            at = slot * 4 + index
            copy = pltpu.make_async_remote_copy(
                src_ref=blended.at[slot, pl.ds(first, rows)],
                dst_ref=stage.at[slot, pl.ds(first, rows)],
                send_sem=send_out.at[at],
                recv_sem=recv_out.at[at],
                device_id=device(-on_h, -on_w, slot),
                device_id_type=MESH,
            )
            copy.start()
            outgoing[slot, index] = copy

    forward(0)
    for load in loads:
        load.wait()
    attend(0)
    for index in range(4):
        twin[0, index].wait_recv()
    attend(1)
    forward(2)
    attend(2)
    for index in range(4):
        twin[2, index].wait_recv()
    attend(3)

    place = lax.broadcasted_iota(jnp.int32, (TOKENS, TOKENS), 1)
    token = lax.broadcasted_iota(jnp.int32, (TOKENS, TOKENS), 0)
    restore = jnp.where(token_of(place) == token, 1.0, 0.0).astype(jnp.bfloat16)
    for slot in range(4):
        for index in range(4):
            if (slot, index) in outgoing:
                outgoing[slot, index].wait_recv()
        columns = pl.ds(pl.multiple_of(device(0, 0, slot)[2] * GROUP, GROUP), GROUP)
        out_ref[:, columns] = jnp.dot(restore, stage[slot], preferred_element_type=jnp.float32).astype(jnp.bfloat16)
    for copy in [*incoming.values(), *twin.values(), *outgoing.values()]:
        copy.wait_send()


def shards(latent, qkv_weight, query_gain, key_gain):
    vmem = pl.BlockSpec(memory_space=pltpu.VMEM)
    anywhere = pl.BlockSpec(memory_space=pltpu.HBM)
    out = pl.pallas_call(
        kernel,
        out_shape=pltpu.VMEM((TOKENS, DEPTH), jnp.bfloat16),
        in_specs=[anywhere] * 4,
        out_specs=vmem,
        scratch_shapes=[
            pltpu.VMEM((ROWS, COLS, DEPTH), jnp.bfloat16),
            pltpu.VMEM((LOCAL_HEADS, DEPTH, GROUP), jnp.bfloat16),
            pltpu.VMEM((1, HEAD), jnp.float32),
            pltpu.VMEM((1, HEAD), jnp.float32),
            pltpu.VMEM((TOKENS, DEPTH), jnp.bfloat16),
            pltpu.VMEM((4, TOKENS, DEPTH), jnp.bfloat16),
            pltpu.VMEM((4, TOKENS, GROUP), jnp.bfloat16),
            pltpu.VMEM((4, TOKENS, GROUP), jnp.bfloat16),
            pltpu.SemaphoreType.DMA((4,)),
            pltpu.SemaphoreType.DMA((8,)),
            pltpu.SemaphoreType.DMA((8,)),
            pltpu.SemaphoreType.DMA((8,)),
            pltpu.SemaphoreType.DMA((8,)),
            pltpu.SemaphoreType.DMA((16,)),
            pltpu.SemaphoreType.DMA((16,)),
        ],
        compiler_params=pltpu.CompilerParams(
            collective_id=0, has_side_effects=True, vmem_limit_bytes=60 * 1024 * 1024
        ),
    )(
        latent.reshape(ROWS, COLS, DEPTH),
        qkv_weight.transpose(1, 0, 2),
        query_gain.reshape(1, HEAD),
        key_gain.reshape(1, HEAD),
    )
    return out.reshape(latent.shape)


def solution(mesh):
    return jax.shard_map(
        shards,
        mesh=mesh,
        in_specs=(P("fsdp", None, "ha", "wa", None), P(None, "fsdp", None), P(), P()),
        out_specs=P("fsdp", None, "ha", "wa", None),
        check_vma=False,
    )
```

```python
import math

import jax
import jax.numpy as jnp
from jax import lax
from jax.experimental import pallas as pl
from jax.experimental.pallas import tpu as pltpu
from jax.sharding import PartitionSpec as P

MESH = pl.DeviceIdType.MESH
HEAD = 128
HALF = 4
LOCAL_HEADS = 3
GROUP = LOCAL_HEADS * HEAD
ROWS = 16
COLS = 8
TOKENS = ROWS * COLS
DEPTH = 1536
R_MAIN, R_TOP, L_MAIN, L_TOP = (0, 48, 0, 1), (48, 16, -1, 1), (64, 48, 0, 0), (112, 16, -1, 0)
PIECES = (R_TOP, R_MAIN, L_TOP, L_MAIN)
COPIES = 26
CHUNKS = ((0, 16, 0, 1), (16, 16, 0, 1), (32, 16, 0, 1), R_TOP)


def token_of(place):
    half, rest = place // 64, place % 64
    row = (rest // 4 + HALF) % ROWS
    return row * COLS + rest % 4 + HALF * (1 - half)


def normalized(part, gain):
    values = part.astype(jnp.float32)
    scale = lax.rsqrt(jnp.mean(values * values, axis=-1, keepdims=True) + 1e-06)
    return (values * scale * gain).astype(jnp.bfloat16)


def kernel(
    latent_hbm, weight_hbm, query_gain_hbm, key_gain_hbm, out_ref,
    latent, weight, query_gain, key_gain, sending, tile, blended, stage,
    load_sems, send_sems, recv_sems,
):
    h, w, s = lax.axis_index("ha"), lax.axis_index("wa"), lax.axis_index("fsdp")
    h_size, w_size = lax.axis_size("ha"), lax.axis_size("wa")

    known = {}

    def device(on_h, on_w, other):
        key = (on_h, on_w, other)
        if key not in known:
            known[key] = locate(*key)
        return known[key]

    def locate(on_h, on_w, other):
        group = s
        if other & 1:
            group = group + 1 - 2 * lax.rem(group, 2)
        if other & 2:
            group = lax.rem(group + 2, 4)
        return (lax.rem(h + on_h + h_size, h_size), lax.rem(w + on_w + w_size, w_size), group)

    load_latent = pltpu.make_async_copy(latent_hbm, latent, load_sems.at[0])
    load_latent.start()

    barrier = pltpu.get_barrier_semaphore()
    givers = [device(0, 0, 1), device(0, 0, 2), device(0, -1, 2), device(1, -1, 2), device(1, 0, 0), device(1, 0, 2)]
    for giver in givers:
        pl.semaphore_signal(barrier, inc=1, device_id=giver, device_id_type=MESH)

    moves = [(query_gain_hbm, query_gain), (key_gain_hbm, key_gain)]
    for head in range(LOCAL_HEADS):
        both, value = pl.ds(2 * HEAD * head, 2 * HEAD), pl.ds(HEAD * (2 * LOCAL_HEADS + head), HEAD)
        moves.append((weight_hbm.at[head, :, pl.ds(0, 2 * HEAD)], weight.at[0, :, both]))
        moves.append((weight_hbm.at[head, :, pl.ds(2 * HEAD, HEAD)], weight.at[0, :, value]))
    loads = [
        pltpu.make_async_copy(source, target, load_sems.at[1 + at]) for at, (source, target) in enumerate(moves)
    ]

    place = lax.broadcasted_iota(jnp.int32, (TOKENS, TOKENS), 0)
    token = lax.broadcasted_iota(jnp.int32, (TOKENS, TOKENS), 1)
    arrange = jnp.where(token_of(place) == token, 1.0, 0.0).astype(jnp.bfloat16)

    load_latent.wait()
    for load in loads:
        load.start()
    mine = latent[...].astype(jnp.float32).reshape(TOKENS, DEPTH).astype(jnp.bfloat16)
    right, left = pl.ds(0, 64), pl.ds(64, 64)
    sending[right] = jnp.dot(arrange[:64], mine, preferred_element_type=jnp.float32).astype(jnp.bfloat16)

    pl.semaphore_wait(barrier, len(givers))

    copies = []

    def send(source, target, rows, to):
        number = len(copies)
        copy = pltpu.make_async_remote_copy(
            src_ref=source.at[rows],
            dst_ref=target.at[rows],
            send_sem=send_sems.at[number],
            recv_sem=recv_sems.at[number],
            device_id=to,
            device_id_type=MESH,
        )
        copy.start()
        copies.append(copy)
        return copy

    def rows_of(piece):
        return pl.ds(piece[0], piece[1])

    right_in = [
        send(sending, tile.at[1], rows_of(chunk), device(chunk[2], chunk[3], 2))
        for chunk in (CHUNKS[3], CHUNKS[0], CHUNKS[1], CHUNKS[2])
    ]
    right_in = [*right_in[1:], right_in[0]]
    sending[left] = jnp.dot(arrange[64:], mine, preferred_element_type=jnp.float32).astype(jnp.bfloat16)
    left_in = [
        send(sending, tile.at[0], rows_of(L_TOP), device(-1, 0, 0)),
        send(sending, tile.at[1], rows_of(L_TOP), device(-1, 0, 2)),
        send(sending, tile.at[1], rows_of(L_MAIN), device(0, 0, 2)),
    ]
    tile[0, rows_of(L_MAIN)] = sending[rows_of(L_MAIN)]

    for load in loads:
        load.wait()
    weight_in = send(weight.at[0], weight.at[1], pl.ds(0, DEPTH), device(0, 0, 1))

    relayed = []
    for chunk, copy in zip(CHUNKS, right_in):
        copy.wait_recv()
        relayed.append(send(tile.at[1], tile.at[0], rows_of(chunk), device(0, 0, 2)))
    for copy in left_in:
        copy.wait_recv()

    spot_q = lax.broadcasted_iota(jnp.int32, (TOKENS, TOKENS), 0)
    spot_k = lax.broadcasted_iota(jnp.int32, (TOKENS, TOKENS), 1)
    together = (spot_q % 64 < 32) == (spot_k % 64 < 32)

    outgoing = {}

    def attend(slot, part):
        tokens = tile[slot]
        raised = []
        for head in range(LOCAL_HEADS):
            both = weight[part, :, 2 * HEAD * head : 2 * HEAD * (head + 1)]
            packed = jnp.dot(tokens, both, preferred_element_type=jnp.float32).astype(jnp.bfloat16)
            queries = normalized(packed[:, :HEAD], query_gain[...])
            keyed = normalized(packed[:, HEAD:], key_gain[...])
            scores = lax.dot_general(
                queries, keyed, (((1,), (1,)), ((), ())), preferred_element_type=jnp.float32
            ) * (1.0 / math.sqrt(HEAD))
            raised.append(jnp.exp(jnp.where(together, scores, -1e30)))
        values = weight[part, :, 2 * HEAD * LOCAL_HEADS :]
        valued = jnp.dot(tokens, values, preferred_element_type=jnp.float32).astype(jnp.bfloat16)
        for head in range(LOCAL_HEADS):
            columns = slice(head * HEAD, (head + 1) * HEAD)
            result = jnp.dot(
                raised[head].astype(jnp.bfloat16), valued[:, columns], preferred_element_type=jnp.float32
            ) / jnp.sum(raised[head], axis=-1, keepdims=True)
            blended[slot, part, :, columns] = result.astype(jnp.bfloat16)
        outgoing[slot, part] = []
        for piece in PIECES:
            rows = rows_of(piece)
            if slot == 0 and piece == L_MAIN:
                stage[0, part, rows] = blended[0, part, rows]
            else:
                to = device(-piece[2], -piece[3], 2 * slot)
                outgoing[slot, part].append(send(blended.at[slot, part], stage.at[slot, part], rows, to))

    attend(1, 0)
    weight_in.wait_recv()
    attend(1, 1)
    for copy in relayed:
        copy.wait_recv()
    attend(0, 0)
    attend(0, 1)

    place = lax.broadcasted_iota(jnp.int32, (TOKENS, TOKENS), 1)
    token = lax.broadcasted_iota(jnp.int32, (TOKENS, TOKENS), 0)
    restore = jnp.where(token_of(place) == token, 1.0, 0.0).astype(jnp.bfloat16)
    for slot, part in ((1, 0), (1, 1), (0, 0), (0, 1)):
        for copy in outgoing[slot, part]:
            copy.wait_recv()
        columns = pl.ds(pl.multiple_of(device(0, 0, 2 * slot + part)[2] * GROUP, GROUP), GROUP)
        rebuilt = jnp.dot(restore, stage[slot, part], preferred_element_type=jnp.float32)
        out_ref[:, columns] = rebuilt.astype(jnp.bfloat16)
    for copy in copies:
        copy.wait_send()


def shards(latent, qkv_weight, query_gain, key_gain):
    vmem = pl.BlockSpec(memory_space=pltpu.VMEM)
    anywhere = pl.BlockSpec(memory_space=pltpu.HBM)
    out = pl.pallas_call(
        kernel,
        out_shape=pltpu.VMEM((TOKENS, DEPTH), jnp.bfloat16),
        in_specs=[anywhere] * 4,
        out_specs=vmem,
        scratch_shapes=[
            pltpu.VMEM((ROWS, COLS, DEPTH), jnp.bfloat16),
            pltpu.VMEM((2, DEPTH, LOCAL_HEADS * GROUP), jnp.bfloat16),
            pltpu.VMEM((1, HEAD), jnp.float32),
            pltpu.VMEM((1, HEAD), jnp.float32),
            pltpu.VMEM((TOKENS, DEPTH), jnp.bfloat16),
            pltpu.VMEM((2, TOKENS, DEPTH), jnp.bfloat16),
            pltpu.VMEM((2, 2, TOKENS, GROUP), jnp.bfloat16),
            pltpu.VMEM((2, 2, TOKENS, GROUP), jnp.bfloat16),
            pltpu.SemaphoreType.DMA((9,)),
            pltpu.SemaphoreType.DMA((COPIES,)),
            pltpu.SemaphoreType.DMA((COPIES,)),
        ],
        compiler_params=pltpu.CompilerParams(
            collective_id=0, has_side_effects=True, vmem_limit_bytes=60 * 1024 * 1024
        ),
    )(
        latent.reshape(ROWS, COLS, DEPTH),
        qkv_weight.transpose(1, 0, 2),
        query_gain.reshape(1, HEAD),
        key_gain.reshape(1, HEAD),
    )
    return out.reshape(latent.shape)


def solution(mesh):
    return jax.shard_map(
        shards,
        mesh=mesh,
        in_specs=(P("fsdp", None, "ha", "wa", None), P(None, "fsdp", None), P(), P()),
        out_specs=P("fsdp", None, "ha", "wa", None),
        check_vma=False,
    )
```

```python
import math

import jax
import jax.numpy as jnp
from jax import lax
from jax.experimental import pallas as pl
from jax.experimental.pallas import tpu as pltpu
from jax.sharding import PartitionSpec as P

MESH = pl.DeviceIdType.MESH
HEAD = 128
HALF = 4
LOCAL_HEADS = 3
GROUP = LOCAL_HEADS * HEAD
ROWS = 16
COLS = 8
TOKENS = ROWS * COLS
DEPTH = 1536
R_MAIN, R_TOP, L_MAIN, L_TOP = (0, 48, 0, 1), (48, 16, -1, 1), (64, 48, 0, 0), (112, 16, -1, 0)
PIECES = (L_TOP, L_MAIN, R_TOP, R_MAIN)
COPIES = 19
CHUNKS = ((0, 16, 0, 1), (16, 16, 0, 1), (32, 16, 0, 1), R_TOP)


def token_of(place):
    half, rest = place // 64, place % 64
    row = (rest // 4 + HALF) % ROWS
    return row * COLS + rest % 4 + HALF * (1 - half)


def normalized(part, gain):
    values = part.astype(jnp.float32)
    scale = lax.rsqrt(jnp.mean(values * values, axis=-1, keepdims=True) + 1e-06)
    return (values * scale * gain).astype(jnp.bfloat16)


def kernel(
    latent_hbm, weight_hbm, query_gain_hbm, key_gain_hbm, out_ref,
    latent, weight, query_gain, key_gain, sending, tile, blended, stage,
    load_sems, send_sems, recv_sems,
):
    h, w, s = lax.axis_index("ha"), lax.axis_index("wa"), lax.axis_index("fsdp")
    h_size, w_size = lax.axis_size("ha"), lax.axis_size("wa")

    known = {}

    def device(on_h, on_w, other):
        key = (on_h, on_w, other)
        if key not in known:
            known[key] = locate(*key)
        return known[key]

    def locate(on_h, on_w, other):
        group = s
        if other & 1:
            group = group + 1 - 2 * lax.rem(group, 2)
        if other & 2:
            group = lax.rem(group + 2, 4)
        return (lax.rem(h + on_h + h_size, h_size), lax.rem(w + on_w + w_size, w_size), group)

    load_latent = pltpu.make_async_copy(latent_hbm, latent, load_sems.at[0])
    load_latent.start()

    barrier = pltpu.get_barrier_semaphore()
    givers = [device(0, 0, 1), device(0, 0, 2), device(0, -1, 2), device(1, -1, 2), device(1, 0, 0), device(1, 0, 2)]
    for giver in givers:
        pl.semaphore_signal(barrier, inc=1, device_id=giver, device_id_type=MESH)

    moves = [(query_gain_hbm, query_gain), (key_gain_hbm, key_gain)]
    for head in range(LOCAL_HEADS):
        both, value = pl.ds(2 * HEAD * head, 2 * HEAD), pl.ds(HEAD * (2 * LOCAL_HEADS + head), HEAD)
        moves.append((weight_hbm.at[head, :, pl.ds(0, 2 * HEAD)], weight.at[0, :, both]))
        moves.append((weight_hbm.at[head, :, pl.ds(2 * HEAD, HEAD)], weight.at[0, :, value]))
    loads = [
        pltpu.make_async_copy(source, target, load_sems.at[1 + at]) for at, (source, target) in enumerate(moves)
    ]

    place = lax.broadcasted_iota(jnp.int32, (TOKENS, TOKENS), 0)
    token = lax.broadcasted_iota(jnp.int32, (TOKENS, TOKENS), 1)
    arrange = jnp.where(token_of(place) == token, 1.0, 0.0).astype(jnp.bfloat16)

    load_latent.wait()
    for load in loads:
        load.start()
    mine = latent[...].astype(jnp.float32).reshape(TOKENS, DEPTH).astype(jnp.bfloat16)
    right, left = pl.ds(0, 64), pl.ds(64, 64)
    sending[right] = jnp.dot(arrange[:64], mine, preferred_element_type=jnp.float32).astype(jnp.bfloat16)

    pl.semaphore_wait(barrier, len(givers))

    copies = []

    def send(source, target, rows, to):
        number = len(copies)
        copy = pltpu.make_async_remote_copy(
            src_ref=source.at[rows],
            dst_ref=target.at[rows],
            send_sem=send_sems.at[number],
            recv_sem=recv_sems.at[number],
            device_id=to,
            device_id_type=MESH,
        )
        copy.start()
        copies.append(copy)
        return copy

    def rows_of(piece):
        return pl.ds(piece[0], piece[1])

    right_in = [
        send(sending, tile.at[1], rows_of(chunk), device(chunk[2], chunk[3], 2))
        for chunk in (CHUNKS[3], CHUNKS[0], CHUNKS[1], CHUNKS[2])
    ]
    right_in = [*right_in[1:], right_in[0]]
    sending[left] = jnp.dot(arrange[64:], mine, preferred_element_type=jnp.float32).astype(jnp.bfloat16)
    left_in = [
        send(sending, tile.at[0], rows_of(L_TOP), device(-1, 0, 0)),
        send(sending, tile.at[1], rows_of(L_TOP), device(-1, 0, 2)),
        send(sending, tile.at[1], rows_of(L_MAIN), device(0, 0, 2)),
    ]
    tile[0, rows_of(L_MAIN)] = sending[rows_of(L_MAIN)]

    for load in loads:
        load.wait()
    weight_in = send(weight.at[0], weight.at[1], pl.ds(0, DEPTH), device(0, 0, 1))

    relayed = []
    for chunk, copy in zip(CHUNKS, right_in):
        copy.wait_recv()
        relayed.append(send(tile.at[1], tile.at[0], rows_of(chunk), device(0, 0, 2)))
    for copy in left_in:
        copy.wait_recv()

    spot_q = lax.broadcasted_iota(jnp.int32, (TOKENS, TOKENS), 0)
    spot_k = lax.broadcasted_iota(jnp.int32, (TOKENS, TOKENS), 1)
    together = (spot_q % 64 < 32) == (spot_k % 64 < 32)

    outgoing = {}

    def attend(slot):
        tokens = tile[slot]
        raised = {}
        for part in range(2):
            for head in range(LOCAL_HEADS):
                both = weight[part, :, 2 * HEAD * head : 2 * HEAD * (head + 1)]
                packed = jnp.dot(tokens, both, preferred_element_type=jnp.float32).astype(jnp.bfloat16)
                queries = normalized(packed[:, :HEAD], query_gain[...])
                keyed = normalized(packed[:, HEAD:], key_gain[...])
                scores = lax.dot_general(
                    queries, keyed, (((1,), (1,)), ((), ())), preferred_element_type=jnp.float32
                ) * (1.0 / math.sqrt(HEAD))
                raised[part, head] = jnp.exp(jnp.where(together, scores, -1e30))
        for part in range(2):
            values = weight[part, :, 2 * HEAD * LOCAL_HEADS :]
            valued = jnp.dot(tokens, values, preferred_element_type=jnp.float32).astype(jnp.bfloat16)
            for head in range(LOCAL_HEADS):
                columns = slice(head * HEAD, (head + 1) * HEAD)
                result = jnp.dot(
                    raised[part, head].astype(jnp.bfloat16), valued[:, columns], preferred_element_type=jnp.float32
                ) / jnp.sum(raised[part, head], axis=-1, keepdims=True)
                blended[slot, :, pl.ds(part * GROUP + head * HEAD, HEAD)] = result.astype(jnp.bfloat16)
        outgoing[slot] = []
        for piece in PIECES:
            rows = rows_of(piece)
            if slot == 0 and piece == L_MAIN:
                stage[0, rows] = blended[0, rows]
            else:
                to = device(-piece[2], -piece[3], 2 * slot)
                outgoing[slot].append(send(blended.at[slot], stage.at[slot], rows, to))

    weight_in.wait_recv()
    attend(1)
    for copy in relayed:
        copy.wait_recv()
    attend(0)

    place = lax.broadcasted_iota(jnp.int32, (TOKENS, TOKENS), 1)
    token = lax.broadcasted_iota(jnp.int32, (TOKENS, TOKENS), 0)
    restore = jnp.where(token_of(place) == token, 1.0, 0.0).astype(jnp.bfloat16)
    for slot in (1, 0):
        for copy in outgoing[slot]:
            copy.wait_recv()
        rebuilt = jnp.dot(restore, stage[slot], preferred_element_type=jnp.float32).astype(jnp.bfloat16)
        for part in range(2):
            columns = pl.ds(pl.multiple_of(device(0, 0, 2 * slot + part)[2] * GROUP, GROUP), GROUP)
            out_ref[:, columns] = rebuilt[:, part * GROUP : (part + 1) * GROUP]
    for copy in copies:
        copy.wait_send()


def shards(latent, qkv_weight, query_gain, key_gain):
    vmem = pl.BlockSpec(memory_space=pltpu.VMEM)
    anywhere = pl.BlockSpec(memory_space=pltpu.HBM)
    out = pl.pallas_call(
        kernel,
        out_shape=pltpu.VMEM((TOKENS, DEPTH), jnp.bfloat16),
        in_specs=[anywhere] * 4,
        out_specs=vmem,
        scratch_shapes=[
            pltpu.VMEM((ROWS, COLS, DEPTH), jnp.bfloat16),
            pltpu.VMEM((2, DEPTH, LOCAL_HEADS * GROUP), jnp.bfloat16),
            pltpu.VMEM((1, HEAD), jnp.float32),
            pltpu.VMEM((1, HEAD), jnp.float32),
            pltpu.VMEM((TOKENS, DEPTH), jnp.bfloat16),
            pltpu.VMEM((2, TOKENS, DEPTH), jnp.bfloat16),
            pltpu.VMEM((2, TOKENS, 2 * GROUP), jnp.bfloat16),
            pltpu.VMEM((2, TOKENS, 2 * GROUP), jnp.bfloat16),
            pltpu.SemaphoreType.DMA((9,)),
            pltpu.SemaphoreType.DMA((COPIES,)),
            pltpu.SemaphoreType.DMA((COPIES,)),
        ],
        compiler_params=pltpu.CompilerParams(
            collective_id=0, has_side_effects=True, vmem_limit_bytes=60 * 1024 * 1024
        ),
    )(
        latent.reshape(ROWS, COLS, DEPTH),
        qkv_weight.transpose(1, 0, 2),
        query_gain.reshape(1, HEAD),
        key_gain.reshape(1, HEAD),
    )
    return out.reshape(latent.shape)


def solution(mesh):
    return jax.shard_map(
        shards,
        mesh=mesh,
        in_specs=(P("fsdp", None, "ha", "wa", None), P(None, "fsdp", None), P(), P()),
        out_specs=P("fsdp", None, "ha", "wa", None),
        check_vma=False,
    )
```

```python
import math

import jax
import jax.numpy as jnp
from jax import lax
from jax.experimental import pallas as pl
from jax.experimental.pallas import tpu as pltpu
from jax.sharding import PartitionSpec as P

MESH = pl.DeviceIdType.MESH
HEAD = 128
HALF = 4
LOCAL_HEADS = 3
GROUP = LOCAL_HEADS * HEAD
ROWS = 16
COLS = 8
TOKENS = ROWS * COLS
DEPTH = 1536
R_MAIN, R_TOP, L_MAIN, L_TOP = (0, 48, 0, 1), (48, 16, -1, 1), (64, 48, 0, 0), (112, 16, -1, 0)
PIECES = (L_TOP, L_MAIN, R_TOP, R_MAIN)
COPIES = 17
CHUNKS = ((0, 32, 0, 1), (32, 16, 0, 1), R_TOP)


def token_of(place):
    half, rest = place // 64, place % 64
    row = (rest // 4 + HALF) % ROWS
    return row * COLS + rest % 4 + HALF * (1 - half)


def normalized(part, gain):
    values = part.astype(jnp.float32)
    scale = lax.rsqrt(jnp.mean(values * values, axis=-1, keepdims=True) + 1e-06)
    return (values * scale * gain).astype(jnp.bfloat16)


def kernel(
    latent_hbm, weight_hbm, query_gain_hbm, key_gain_hbm, out_ref,
    latent, weight, query_gain, key_gain, sending, tile, blended, stage,
    load_sems, send_sems, recv_sems,
):
    h, w, s = lax.axis_index("ha"), lax.axis_index("wa"), lax.axis_index("fsdp")
    h_size, w_size = lax.axis_size("ha"), lax.axis_size("wa")

    known = {}

    def device(on_h, on_w, other):
        key = (on_h, on_w, other)
        if key not in known:
            known[key] = locate(*key)
        return known[key]

    def locate(on_h, on_w, other):
        group = s
        if other & 1:
            group = group + 1 - 2 * lax.rem(group, 2)
        if other & 2:
            group = lax.rem(group + 2, 4)
        return (lax.rem(h + on_h + h_size, h_size), lax.rem(w + on_w + w_size, w_size), group)

    load_latent = pltpu.make_async_copy(latent_hbm, latent, load_sems.at[0])
    load_latent.start()

    barrier = pltpu.get_barrier_semaphore()
    givers = [device(0, 0, 1), device(0, 0, 2), device(0, -1, 2), device(1, -1, 2), device(1, 0, 0), device(1, 0, 2)]
    for giver in givers:
        pl.semaphore_signal(barrier, inc=1, device_id=giver, device_id_type=MESH)

    moves = [(query_gain_hbm, query_gain), (key_gain_hbm, key_gain)]
    for head in range(LOCAL_HEADS):
        both, value = pl.ds(2 * HEAD * head, 2 * HEAD), pl.ds(HEAD * (2 * LOCAL_HEADS + head), HEAD)
        moves.append((weight_hbm.at[head, :, pl.ds(0, 2 * HEAD)], weight.at[0, :, both]))
        moves.append((weight_hbm.at[head, :, pl.ds(2 * HEAD, HEAD)], weight.at[0, :, value]))
    loads = [
        pltpu.make_async_copy(source, target, load_sems.at[1 + at]) for at, (source, target) in enumerate(moves)
    ]

    place = lax.broadcasted_iota(jnp.int32, (TOKENS, TOKENS), 0)
    token = lax.broadcasted_iota(jnp.int32, (TOKENS, TOKENS), 1)
    arrange = jnp.where(token_of(place) == token, 1.0, 0.0).astype(jnp.bfloat16)

    load_latent.wait()
    for load in loads:
        load.start()
    mine = latent[...].astype(jnp.float32).reshape(TOKENS, DEPTH).astype(jnp.bfloat16)
    right, left = pl.ds(0, 64), pl.ds(64, 64)
    sending[right] = jnp.dot(arrange[:64], mine, preferred_element_type=jnp.float32).astype(jnp.bfloat16)

    pl.semaphore_wait(barrier, len(givers))

    copies = []

    def send(source, target, rows, to):
        number = len(copies)
        copy = pltpu.make_async_remote_copy(
            src_ref=source.at[rows],
            dst_ref=target.at[rows],
            send_sem=send_sems.at[number],
            recv_sem=recv_sems.at[number],
            device_id=to,
            device_id_type=MESH,
        )
        copy.start()
        copies.append(copy)
        return copy

    def rows_of(piece):
        return pl.ds(piece[0], piece[1])

    right_in = [
        send(sending, tile.at[1], rows_of(chunk), device(chunk[2], chunk[3], 2))
        for chunk in (CHUNKS[-1], *CHUNKS[:-1])
    ]
    right_in = [*right_in[1:], right_in[0]]
    sending[left] = jnp.dot(arrange[64:], mine, preferred_element_type=jnp.float32).astype(jnp.bfloat16)
    left_in = [
        send(sending, tile.at[0], rows_of(L_TOP), device(-1, 0, 0)),
        send(sending, tile.at[1], rows_of(L_TOP), device(-1, 0, 2)),
        send(sending, tile.at[1], rows_of(L_MAIN), device(0, 0, 2)),
    ]
    tile[0, rows_of(L_MAIN)] = sending[rows_of(L_MAIN)]

    for load in loads:
        load.wait()
    weight_in = send(weight.at[0], weight.at[1], pl.ds(0, DEPTH), device(0, 0, 1))

    relayed = []
    for chunk, copy in zip(CHUNKS, right_in):
        copy.wait_recv()
        relayed.append(send(tile.at[1], tile.at[0], rows_of(chunk), device(0, 0, 2)))
    for copy in left_in:
        copy.wait_recv()

    spot_q = lax.broadcasted_iota(jnp.int32, (TOKENS, TOKENS), 0)
    spot_k = lax.broadcasted_iota(jnp.int32, (TOKENS, TOKENS), 1)
    together = (spot_q % 64 < 32) == (spot_k % 64 < 32)

    outgoing = {}

    def attend(slot):
        tokens = tile[slot]
        raised = {}
        for part in range(2):
            for head in range(LOCAL_HEADS):
                both = weight[part, :, 2 * HEAD * head : 2 * HEAD * (head + 1)]
                packed = jnp.dot(tokens, both, preferred_element_type=jnp.float32).astype(jnp.bfloat16)
                queries = normalized(packed[:, :HEAD], query_gain[...])
                keyed = normalized(packed[:, HEAD:], key_gain[...])
                scores = lax.dot_general(
                    queries, keyed, (((1,), (1,)), ((), ())), preferred_element_type=jnp.float32
                ) * (1.0 / math.sqrt(HEAD))
                raised[part, head] = jnp.exp(jnp.where(together, scores, -1e30))
        for part in range(2):
            values = weight[part, :, 2 * HEAD * LOCAL_HEADS :]
            valued = jnp.dot(tokens, values, preferred_element_type=jnp.float32).astype(jnp.bfloat16)
            for head in range(LOCAL_HEADS):
                columns = slice(head * HEAD, (head + 1) * HEAD)
                result = jnp.dot(
                    raised[part, head].astype(jnp.bfloat16), valued[:, columns], preferred_element_type=jnp.float32
                ) / jnp.sum(raised[part, head], axis=-1, keepdims=True)
                blended[slot, :, pl.ds(part * GROUP + head * HEAD, HEAD)] = result.astype(jnp.bfloat16)
        outgoing[slot] = []
        for piece in PIECES:
            rows = rows_of(piece)
            if slot == 0 and piece == L_MAIN:
                stage[0, rows] = blended[0, rows]
            else:
                to = device(-piece[2], -piece[3], 2 * slot)
                outgoing[slot].append(send(blended.at[slot], stage.at[slot], rows, to))

    weight_in.wait_recv()
    attend(1)
    for copy in relayed:
        copy.wait_recv()
    attend(0)

    place = lax.broadcasted_iota(jnp.int32, (TOKENS, TOKENS), 1)
    token = lax.broadcasted_iota(jnp.int32, (TOKENS, TOKENS), 0)
    restore = jnp.where(token_of(place) == token, 1.0, 0.0).astype(jnp.bfloat16)
    for slot in (1, 0):
        for copy in outgoing[slot]:
            copy.wait_recv()
        rebuilt = jnp.dot(restore, stage[slot], preferred_element_type=jnp.float32).astype(jnp.bfloat16)
        for part in range(2):
            columns = pl.ds(pl.multiple_of(device(0, 0, 2 * slot + part)[2] * GROUP, GROUP), GROUP)
            out_ref[:, columns] = rebuilt[:, part * GROUP : (part + 1) * GROUP]
    for copy in copies:
        copy.wait_send()


def shards(latent, qkv_weight, query_gain, key_gain):
    vmem = pl.BlockSpec(memory_space=pltpu.VMEM)
    anywhere = pl.BlockSpec(memory_space=pltpu.HBM)
    out = pl.pallas_call(
        kernel,
        out_shape=pltpu.VMEM((TOKENS, DEPTH), jnp.bfloat16),
        in_specs=[anywhere] * 4,
        out_specs=vmem,
        scratch_shapes=[
            pltpu.VMEM((ROWS, COLS, DEPTH), jnp.bfloat16),
            pltpu.VMEM((2, DEPTH, LOCAL_HEADS * GROUP), jnp.bfloat16),
            pltpu.VMEM((1, HEAD), jnp.float32),
            pltpu.VMEM((1, HEAD), jnp.float32),
            pltpu.VMEM((TOKENS, DEPTH), jnp.bfloat16),
            pltpu.VMEM((2, TOKENS, DEPTH), jnp.bfloat16),
            pltpu.VMEM((2, TOKENS, 2 * GROUP), jnp.bfloat16),
            pltpu.VMEM((2, TOKENS, 2 * GROUP), jnp.bfloat16),
            pltpu.SemaphoreType.DMA((9,)),
            pltpu.SemaphoreType.DMA((COPIES,)),
            pltpu.SemaphoreType.DMA((COPIES,)),
        ],
        compiler_params=pltpu.CompilerParams(
            collective_id=0, has_side_effects=True, vmem_limit_bytes=60 * 1024 * 1024
        ),
    )(
        latent.reshape(ROWS, COLS, DEPTH),
        qkv_weight.transpose(1, 0, 2),
        query_gain.reshape(1, HEAD),
        key_gain.reshape(1, HEAD),
    )
    return out.reshape(latent.shape)


def solution(mesh):
    return jax.shard_map(
        shards,
        mesh=mesh,
        in_specs=(P("fsdp", None, "ha", "wa", None), P(None, "fsdp", None), P(), P()),
        out_specs=P("fsdp", None, "ha", "wa", None),
        check_vma=False,
    )
```
